32 devices in a mesh: seq: 8 (over z, x), head: 4 (over y, core).
Axes of the slice: x: 2, y: 2, z: 4, core: 2. Of those that a mesh axis runs over, the one named last changes fastest.
Arguments:
- tokens: bfloat16 [2048, 4096], P('seq'), may hold values from -6 to 6
- w_query: bfloat16 [4096, 4096], P('seq', 'head'), may hold values from -0.09375 to 0.09375
- w_key: bfloat16 [4096, 4096], P('seq', 'head'), may hold values from -0.09375 to 0.09375
- w_value: bfloat16 [4096, 4096], P('seq', 'head'), may hold values from -0.09375 to 0.09375
- grad_out: bfloat16 [2048, 4096], P('seq', 'head'), may hold values from -6 to 6
Outputs:
- attn_out: bfloat16 [2048, 4096], P('seq', 'head')
- grad_x: bfloat16 [2048, 4096], P('seq', 'head')
- grad_wq: bfloat16 [4096, 4096], P('seq', 'head')
- grad_wk: bfloat16 [4096, 4096], P('seq', 'head')
- grad_wv: bfloat16 [4096, 4096], P('seq', 'head')
The draws below stay inside these ranges and needn't reach their ends.
All inputs are finite; a program needn't handle non-finite values.
Results may differ from the reference program's by a relative error of at most 0.017.
Values may be sent and summed in bfloat16 or wider, within the bound.
A program may use at most 192 MiB of HBM per device.

```python
import math
import jax
import jax.numpy as jnp
from jax import lax

D = 4096
H = 32
HD = 128
BLOCK = 128
TOK_DEV = 256
TOKENS = 2048
N_SEQ = 8
N_HEAD = 4


def strengthened(drawn, key, source, target, parts, factor):
    def block_of(axis_at):
        return (jnp.arange(drawn.shape[axis_at]) // (drawn.shape[axis_at] // parts)).reshape((-1,) + (1,) * (drawn.ndim - 1 - axis_at))

    first = jax.random.permutation(key, parts)[block_of(target)]
    second = (block_of(target) + parts // 2) % parts
    return jnp.where((block_of(source) == first) | (block_of(source) == second), factor * drawn, drawn)


def block_levels(own_key, extent, pieces, low, largest):
    def one(axis_at, shards_of):
        draws = jax.random.uniform(jax.random.fold_in(jax.random.fold_in(own_key, 6), axis_at), (shards_of,), jnp.float32, low / len(pieces), largest / len(pieces))
        return jnp.repeat(jnp.exp(draws), extent[axis_at] // shards_of).reshape((-1,) + (1,) * (len(extent) - axis_at - 1))

    gain = one(*pieces[0])
    for cut in pieces[1:]:
        gain = gain * one(*cut)
    return gain


def scatter_about(own_key, shape, spread, limit, split=(), held_as=jnp.bfloat16):
    result = jax.random.normal(own_key, shape, jnp.float32) * spread
    if len(split) > 0:
        result = block_levels(own_key, shape, split, -0.22, 0.18) * result
    return jnp.clip(result, min=-limit, max=limit).astype(held_as)


def gaussian_with(own_key, shape, scale, reach, cuts, heavy, dtype=jnp.bfloat16):
    result = scale * jax.random.normal(own_key, shape, jnp.float32)
    if cuts:
        result = result * block_levels(own_key, shape, cuts, -0.22, 0.18)
    return jnp.clip(strengthened(result, jax.random.fold_in(own_key, 3), *heavy), -reach, reach).astype(dtype)


def setup_inputs(seed: int = 0) -> dict:
    splits = jax.random.split(jax.random.key(seed), 6)
    tokens = gaussian_with(splits[0], (TOKENS, D), 1.0, 6.0, ((0, 8),), (0, 1, 8, 2.0))
    w_query = scatter_about(splits[1], (D, H * HD), D ** -0.5, 0.09375, ((0, 8), (1, 4)))
    w_key = scatter_about(splits[2], (D, H * HD), D ** -0.5, 0.09375, ((0, 8), (1, 4)))
    w_value = scatter_about(splits[3], (D, H * HD), D ** -0.5, 0.09375, ((0, 8), (1, 4)))
    grad_out = scatter_about(splits[4], (TOKENS, H * HD), 1.0, 6.0, ((0, 8), (1, 4)))
    return {"tokens": tokens, "w_query": w_query, "w_key": w_key, "w_value": w_value, "grad_out": grad_out}


def split_blocks(matrix):
    return matrix.reshape(matrix.shape[0] // BLOCK, BLOCK, H, HD).astype(jnp.float32)

def reference(tokens, w_query, w_key, w_value, grad_out):
    score_scale = 1.0 / math.sqrt(HD * TOKENS)
    queries = jnp.dot(tokens, w_query, preferred_element_type=jnp.float32).astype(jnp.bfloat16)
    keys_all = jnp.dot(tokens, w_key, preferred_element_type=jnp.float32).astype(jnp.bfloat16)
    values_all = jnp.dot(tokens, w_value, preferred_element_type=jnp.float32).astype(jnp.bfloat16)
    q_blocks = split_blocks(queries)
    k_blocks = split_blocks(keys_all)
    v_blocks = split_blocks(values_all)
    g_blocks = split_blocks(grad_out)
    kv_block = jnp.einsum('bthd,bthe->bhde', k_blocks, v_blocks)
    qg_block = jnp.einsum('bthd,bthe->bhde', q_blocks, g_blocks)
    zero_block = jnp.zeros_like(kv_block[:1])
    prefix_state = jnp.concatenate([zero_block, jnp.cumsum(kv_block, axis=0)[:-1]], axis=0)
    suffix_run = jnp.cumsum(qg_block[::-1], axis=0)[::-1]
    suffix_state = jnp.concatenate([suffix_run[1:], zero_block], axis=0)
    prefix_state = prefix_state.astype(jnp.bfloat16).astype(jnp.float32)
    suffix_state = suffix_state.astype(jnp.bfloat16).astype(jnp.float32)
    causal_mask = lax.broadcasted_iota(jnp.int32, (BLOCK, BLOCK), 0) >= lax.broadcasted_iota(jnp.int32, (BLOCK, BLOCK), 1)
    raw_scores = jnp.einsum('bthd,bshd->bhts', q_blocks, k_blocks)
    scores = jnp.where(causal_mask, raw_scores * score_scale, 0.0).astype(jnp.bfloat16).astype(jnp.float32)
    intra = jnp.einsum('bhts,bshe->bthe', scores, v_blocks)
    carried = jnp.einsum('bthd,bhde->bthe', q_blocks, prefix_state)
    attn_out = (intra + score_scale * carried).astype(jnp.bfloat16).reshape(TOKENS, H * HD)
    raw_grad = jnp.einsum('bthe,bshe->bhts', g_blocks, v_blocks)
    grad_scores = jnp.where(causal_mask, raw_grad * score_scale, 0.0).astype(jnp.bfloat16).astype(jnp.float32)
    grad_q = jnp.einsum('bhts,bshd->bthd', grad_scores, k_blocks) + score_scale * jnp.einsum('bthe,bhde->bthd', g_blocks, prefix_state)
    grad_k = jnp.einsum('bhts,bthd->bshd', grad_scores, q_blocks) + score_scale * jnp.einsum('bshe,bhde->bshd', v_blocks, suffix_state)
    grad_v = jnp.einsum('bhts,bthe->bshe', scores, g_blocks) + score_scale * jnp.einsum('bshd,bhde->bshe', k_blocks, suffix_state)
    grad_q = grad_q.astype(jnp.bfloat16).reshape(TOKENS, H * HD)
    grad_k = grad_k.astype(jnp.bfloat16).reshape(TOKENS, H * HD)
    grad_v = grad_v.astype(jnp.bfloat16).reshape(TOKENS, H * HD)
    group_cols = H * HD // N_HEAD
    input_total = jnp.zeros((TOKENS, D), jnp.float32)
    for group in range(N_HEAD):
        lower = group * group_cols
        upper = lower + group_cols
        term = jnp.dot(grad_q[:, lower:upper], w_query[:, lower:upper].T, preferred_element_type=jnp.float32)
        term = term + jnp.dot(grad_k[:, lower:upper], w_key[:, lower:upper].T, preferred_element_type=jnp.float32)
        term = term + jnp.dot(grad_v[:, lower:upper], w_value[:, lower:upper].T, preferred_element_type=jnp.float32)
        input_total = input_total + lax.optimization_barrier(term.astype(jnp.bfloat16)).astype(jnp.float32)
    grad_x = input_total.astype(jnp.bfloat16)

    def add_group(index, totals):
        start = (index * TOK_DEV).astype(jnp.int32)
        token_rows = lax.dynamic_slice_in_dim(tokens, start, TOK_DEV, 0)
        updated = []
        for total, gradient in zip(totals, (grad_q, grad_k, grad_v)):
            grad_rows = lax.dynamic_slice_in_dim(gradient, start, TOK_DEV, 0)
            term = jnp.dot(token_rows.T, grad_rows, preferred_element_type=jnp.float32)
            updated.append(total + lax.optimization_barrier(term.astype(jnp.bfloat16)).astype(jnp.float32))
        return tuple(updated)
    zero_weight = jnp.zeros((D, H * HD), jnp.float32)
    totals = lax.fori_loop(0, N_SEQ, add_group, (zero_weight, zero_weight, zero_weight))
    return (attn_out, grad_x, totals[0].astype(jnp.bfloat16), totals[1].astype(jnp.bfloat16), totals[2].astype(jnp.bfloat16))
```

```python
import math

import jax
import jax.numpy as jnp
from jax import lax
from jax.sharding import PartitionSpec as P

HD = 128
BLOCK = 128


def prefix(value, axis, join, neutral, backward):
    count = lax.axis_size(axis)
    place = lax.axis_index(axis)
    ahead = count - 1 - place if backward else place
    gathered = lax.all_gather(value.astype(jnp.bfloat16), axis)
    state = jnp.zeros_like(value) + jnp.asarray(neutral, value.dtype)

    def one(lap, state):
        source = count - 1 - lap if backward else lap
        return join(state, lax.dynamic_index_in_dim(gathered, source, 0, False).astype(value.dtype))

    return lax.fori_loop(0, ahead, one, state)


def add_states(earlier, later):
    return jax.tree.map(jnp.add, earlier, later)


def split_blocks(matrix, head_count):
    return matrix.reshape(matrix.shape[0] // BLOCK, BLOCK, head_count, HD)


def before_blocks(blocks, carried):
    running = jnp.cumsum(blocks, axis=0)
    return carried[None] + jnp.concatenate([jnp.zeros_like(blocks[:1]), running[:-1]], axis=0)


def after_blocks(blocks, carried):
    running = jnp.cumsum(blocks[::-1], axis=0)[::-1]
    return carried[None] + jnp.concatenate([running[1:], jnp.zeros_like(blocks[:1])], axis=0)


def per_device(tokens, w_query, w_key, w_value, grad_out):
    tok_rows = tokens.shape[0]
    col_count = w_query.shape[1]
    head_count = col_count // HD
    seq_count = lax.axis_size("seq")
    score_scale = 1.0 / math.sqrt(HD * tok_rows * seq_count)
    full_query, full_key, full_value = (
        lax.all_gather(w_query, "seq", axis=0, tiled=True),
        lax.all_gather(w_key, "seq", axis=0, tiled=True),
        lax.all_gather(w_value, "seq", axis=0, tiled=True),
    )
    queries = jnp.dot(tokens, full_query, preferred_element_type=jnp.float32).astype(jnp.bfloat16)
    keys_all = jnp.dot(tokens, full_key, preferred_element_type=jnp.float32).astype(jnp.bfloat16)
    values_all = jnp.dot(tokens, full_value, preferred_element_type=jnp.float32).astype(
        jnp.bfloat16
    )
    q_blocks = split_blocks(queries, head_count)
    k_blocks = split_blocks(keys_all, head_count)
    v_blocks = split_blocks(values_all, head_count)
    g_blocks = split_blocks(grad_out, head_count)
    kv_blocks = jnp.einsum(
        "bthd,bthe->bhde", k_blocks, v_blocks, preferred_element_type=jnp.float32
    )
    qg_blocks = jnp.einsum(
        "bthd,bthe->bhde", q_blocks, g_blocks, preferred_element_type=jnp.float32
    )
    kv_local = jnp.sum(kv_blocks, axis=0)
    qg_local = jnp.sum(qg_blocks, axis=0)
    zero_state = jnp.zeros_like(kv_local)
    kv_before = prefix(kv_local, "seq", add_states, zero_state, False)
    qg_after = prefix(qg_local, "seq", add_states, zero_state, True)
    prefix_state = before_blocks(kv_blocks, kv_before).astype(jnp.bfloat16)
    suffix_state = after_blocks(qg_blocks, qg_after).astype(jnp.bfloat16)
    causal_mask = lax.broadcasted_iota(jnp.int32, (BLOCK, BLOCK), 0) >= lax.broadcasted_iota(
        jnp.int32, (BLOCK, BLOCK), 1
    )
    raw_scores = jnp.einsum(
        "bthd,bshd->bhts", q_blocks, k_blocks, preferred_element_type=jnp.float32
    )
    scores = jnp.where(causal_mask, raw_scores * score_scale, 0.0).astype(jnp.bfloat16)
    intra = jnp.einsum("bhts,bshe->bthe", scores, v_blocks, preferred_element_type=jnp.float32)
    carried = jnp.einsum(
        "bthd,bhde->bthe", q_blocks, prefix_state, preferred_element_type=jnp.float32
    )
    attn_out = (intra + score_scale * carried).astype(jnp.bfloat16).reshape(tok_rows, col_count)
    raw_grad = jnp.einsum("bthe,bshe->bhts", g_blocks, v_blocks, preferred_element_type=jnp.float32)
    grad_scores = jnp.where(causal_mask, raw_grad * score_scale, 0.0).astype(jnp.bfloat16)
    grad_q = jnp.einsum(
        "bhts,bshd->bthd", grad_scores, k_blocks, preferred_element_type=jnp.float32
    ) + score_scale * jnp.einsum(
        "bthe,bhde->bthd", g_blocks, prefix_state, preferred_element_type=jnp.float32
    )
    grad_k = jnp.einsum(
        "bhts,bthd->bshd", grad_scores, q_blocks, preferred_element_type=jnp.float32
    ) + score_scale * jnp.einsum(
        "bshe,bhde->bshd", v_blocks, suffix_state, preferred_element_type=jnp.float32
    )
    grad_v = jnp.einsum(
        "bhts,bthe->bshe", scores, g_blocks, preferred_element_type=jnp.float32
    ) + score_scale * jnp.einsum(
        "bshd,bhde->bshe", k_blocks, suffix_state, preferred_element_type=jnp.float32
    )
    grad_q = grad_q.astype(jnp.bfloat16).reshape(tok_rows, col_count)
    grad_k = grad_k.astype(jnp.bfloat16).reshape(tok_rows, col_count)
    grad_v = grad_v.astype(jnp.bfloat16).reshape(tok_rows, col_count)
    partial_input = jnp.einsum("tc,dc->td", grad_q, full_query, preferred_element_type=jnp.float32)
    partial_input = partial_input + jnp.einsum(
        "tc,dc->td", grad_k, full_key, preferred_element_type=jnp.float32
    )
    partial_input = partial_input + jnp.einsum(
        "tc,dc->td", grad_v, full_value, preferred_element_type=jnp.float32
    )
    grad_x = lax.psum_scatter(
        partial_input.astype(jnp.bfloat16), "head", scatter_dimension=1, tiled=True
    )
    term_query = jnp.einsum("td,tc->dc", tokens, grad_q, preferred_element_type=jnp.float32)
    term_key = jnp.einsum("td,tc->dc", tokens, grad_k, preferred_element_type=jnp.float32)
    term_value = jnp.einsum("td,tc->dc", tokens, grad_v, preferred_element_type=jnp.float32)
    sum_query, sum_key, sum_value = (
        lax.psum_scatter(
            term_query.astype(jnp.bfloat16), "seq", scatter_dimension=0, tiled=True
        ).astype(jnp.float32),
        lax.psum_scatter(
            term_key.astype(jnp.bfloat16), "seq", scatter_dimension=0, tiled=True
        ).astype(jnp.float32),
        lax.psum_scatter(
            term_value.astype(jnp.bfloat16), "seq", scatter_dimension=0, tiled=True
        ).astype(jnp.float32),
    )
    grad_wq = sum_query.astype(jnp.bfloat16)
    grad_wk = sum_key.astype(jnp.bfloat16)
    grad_wv = sum_value.astype(jnp.bfloat16)
    return (attn_out, grad_x, grad_wq, grad_wk, grad_wv)


def head_attention(queries, keys, values, grads, score_scale):
    head_count = queries.shape[1] // HD
    q_blocks = split_blocks(queries, head_count)
    k_blocks = split_blocks(keys, head_count)
    v_blocks = split_blocks(values, head_count)
    g_blocks = split_blocks(grads, head_count)
    f32 = jnp.float32
    kv_blocks = jnp.einsum("bthd,bthe->bhde", k_blocks, v_blocks, preferred_element_type=f32)
    qg_blocks = jnp.einsum("bthd,bthe->bhde", q_blocks, g_blocks, preferred_element_type=f32)
    zero_state = jnp.zeros_like(kv_blocks[0])
    prefix_state = before_blocks(kv_blocks, zero_state).astype(jnp.bfloat16)
    suffix_state = after_blocks(qg_blocks, zero_state).astype(jnp.bfloat16)
    causal_mask = lax.broadcasted_iota(jnp.int32, (BLOCK, BLOCK), 0) >= lax.broadcasted_iota(
        jnp.int32, (BLOCK, BLOCK), 1
    )
    raw_scores = jnp.einsum("bthd,bshd->bhts", q_blocks, k_blocks, preferred_element_type=f32)
    scores = jnp.where(causal_mask, raw_scores * score_scale, 0.0).astype(jnp.bfloat16)
    raw_grad = jnp.einsum("bthe,bshe->bhts", g_blocks, v_blocks, preferred_element_type=f32)
    grad_scores = jnp.where(causal_mask, raw_grad * score_scale, 0.0).astype(jnp.bfloat16)

    def close(within, across):
        return (within + score_scale * across).astype(jnp.bfloat16).reshape(queries.shape)

    attn_out = close(
        jnp.einsum("bhts,bshe->bthe", scores, v_blocks, preferred_element_type=f32),
        jnp.einsum("bthd,bhde->bthe", q_blocks, prefix_state, preferred_element_type=f32),
    )
    grad_q = close(
        jnp.einsum("bhts,bshd->bthd", grad_scores, k_blocks, preferred_element_type=f32),
        jnp.einsum("bthe,bhde->bthd", g_blocks, prefix_state, preferred_element_type=f32),
    )
    grad_k = close(
        jnp.einsum("bhts,bthd->bshd", grad_scores, q_blocks, preferred_element_type=f32),
        jnp.einsum("bshe,bhde->bshd", v_blocks, suffix_state, preferred_element_type=f32),
    )
    grad_v = close(
        jnp.einsum("bhts,bthe->bshe", scores, g_blocks, preferred_element_type=f32),
        jnp.einsum("bshd,bhde->bshe", k_blocks, suffix_state, preferred_element_type=f32),
    )
    return attn_out, grad_q, grad_k, grad_v


def columns_first(matrix, parts):
    return jnp.transpose(matrix.reshape(matrix.shape[0], parts, -1), (1, 0, 2))


def columns_last(pieces):
    return jnp.transpose(pieces, (1, 0, 2)).reshape(pieces.shape[1], -1)


def per_head(tokens, w_query, w_key, w_value, grad_out):
    seq_count, head_axis = lax.axis_size("seq"), lax.axis_size("head")
    tok_rows, width = tokens.shape
    weight_rows, col_count = w_query.shape
    own = col_count // seq_count
    score_scale = 1.0 / math.sqrt(HD * tok_rows * seq_count)
    share = tok_rows // head_axis
    mine = lax.dynamic_slice_in_dim(tokens, lax.axis_index("head") * share, share, 0)
    every = lax.all_gather(mine, ("seq", "head"), axis=0, tiled=True)
    weights = jnp.concatenate(
        [columns_first(w, seq_count) for w in (w_query, w_key, w_value)], axis=2
    )
    weights = lax.all_to_all(weights, "seq", 0, 0, tiled=True).reshape(width, 3 * own)
    grads = lax.all_to_all(columns_first(grad_out, seq_count), "seq", 0, 0, tiled=True)
    grads = grads.reshape(tok_rows * seq_count, own)
    projected = jnp.dot(every, weights, preferred_element_type=jnp.float32).astype(jnp.bfloat16)
    attn_out, grad_q, grad_k, grad_v = head_attention(
        projected[:, :own], projected[:, own : 2 * own], projected[:, 2 * own :], grads, score_scale
    )
    attn_out = columns_last(
        lax.all_to_all(attn_out.reshape(seq_count, tok_rows, own), "seq", 0, 0, tiled=True)
    )
    gradient = jnp.concatenate([grad_q, grad_k, grad_v], axis=1)
    partial_input = jnp.einsum("tc,dc->td", gradient, weights, preferred_element_type=jnp.float32)
    grad_x = lax.psum_scatter(
        partial_input.astype(jnp.bfloat16), "head", scatter_dimension=1, tiled=True
    )
    grad_x = lax.psum_scatter(grad_x, "seq", scatter_dimension=0, tiled=True)
    grad_w = jnp.einsum("td,tc->dc", every, gradient, preferred_element_type=jnp.float32)
    grad_w = lax.all_to_all(
        grad_w.astype(jnp.bfloat16).reshape(seq_count, weight_rows, 3 * own), "seq", 0, 0, tiled=True
    )
    grad_wq, grad_wk, grad_wv = (
        columns_last(grad_w[:, :, i * own : (i + 1) * own]) for i in range(3)
    )
    return (attn_out, grad_x, grad_wq, grad_wk, grad_wv)


def solution(mesh):
    in_specs = (
        P("seq", None),
        P("seq", "head"),
        P("seq", "head"),
        P("seq", "head"),
        P("seq", "head"),
    )
    out_specs = (
        P("seq", "head"),
        P("seq", "head"),
        P("seq", "head"),
        P("seq", "head"),
        P("seq", "head"),
    )

    def whole(tokens, w_query, w_key, w_value, grad_out):
        seq_count, head_axis = mesh.shape["seq"], mesh.shape["head"]
        heads = w_query.shape[1] // HD
        even = heads % (seq_count * head_axis) == 0 and tokens.shape[0] % (seq_count * head_axis) == 0
        return mapped(per_head if even else per_device)(tokens, w_query, w_key, w_value, grad_out)

    def mapped(body):
        return jax.shard_map(
            body, mesh=mesh, in_specs=in_specs, out_specs=out_specs, check_vma=False
        )

    return whole
```

```python
import math

import jax
import jax.numpy as jnp
from jax import lax
from jax.sharding import PartitionSpec as P

HD = 128
BLOCK = 128


def prefix(value, axis, join, neutral, backward):
    count = lax.axis_size(axis)
    place = lax.axis_index(axis)
    ahead = count - 1 - place if backward else place
    gathered = lax.all_gather(value.astype(jnp.bfloat16), axis)
    state = jnp.zeros_like(value) + jnp.asarray(neutral, value.dtype)

    def one(lap, state):
        source = count - 1 - lap if backward else lap
        return join(state, lax.dynamic_index_in_dim(gathered, source, 0, False).astype(value.dtype))

    return lax.fori_loop(0, ahead, one, state)


def add_states(earlier, later):
    return jax.tree.map(jnp.add, earlier, later)


def split_blocks(matrix, head_count):
    return matrix.reshape(matrix.shape[0] // BLOCK, BLOCK, head_count, HD)


def before_blocks(blocks, carried):
    running = jnp.cumsum(blocks, axis=0)
    return carried[None] + jnp.concatenate([jnp.zeros_like(blocks[:1]), running[:-1]], axis=0)


def after_blocks(blocks, carried):
    running = jnp.cumsum(blocks[::-1], axis=0)[::-1]
    return carried[None] + jnp.concatenate([running[1:], jnp.zeros_like(blocks[:1])], axis=0)


def per_device(tokens, w_query, w_key, w_value, grad_out):
    tok_rows = tokens.shape[0]
    col_count = w_query.shape[1]
    head_count = col_count // HD
    seq_count = lax.axis_size("seq")
    score_scale = 1.0 / math.sqrt(HD * tok_rows * seq_count)
    full_query, full_key, full_value = (
        lax.all_gather(w_query, "seq", axis=0, tiled=True),
        lax.all_gather(w_key, "seq", axis=0, tiled=True),
        lax.all_gather(w_value, "seq", axis=0, tiled=True),
    )
    queries = jnp.dot(tokens, full_query, preferred_element_type=jnp.float32).astype(jnp.bfloat16)
    keys_all = jnp.dot(tokens, full_key, preferred_element_type=jnp.float32).astype(jnp.bfloat16)
    values_all = jnp.dot(tokens, full_value, preferred_element_type=jnp.float32).astype(
        jnp.bfloat16
    )
    q_blocks = split_blocks(queries, head_count)
    k_blocks = split_blocks(keys_all, head_count)
    v_blocks = split_blocks(values_all, head_count)
    g_blocks = split_blocks(grad_out, head_count)
    kv_blocks = jnp.einsum(
        "bthd,bthe->bhde", k_blocks, v_blocks, preferred_element_type=jnp.float32
    )
    qg_blocks = jnp.einsum(
        "bthd,bthe->bhde", q_blocks, g_blocks, preferred_element_type=jnp.float32
    )
    kv_local = jnp.sum(kv_blocks, axis=0)
    qg_local = jnp.sum(qg_blocks, axis=0)
    zero_state = jnp.zeros_like(kv_local)
    kv_before = prefix(kv_local, "seq", add_states, zero_state, False)
    qg_after = prefix(qg_local, "seq", add_states, zero_state, True)
    prefix_state = before_blocks(kv_blocks, kv_before).astype(jnp.bfloat16)
    suffix_state = after_blocks(qg_blocks, qg_after).astype(jnp.bfloat16)
    causal_mask = lax.broadcasted_iota(jnp.int32, (BLOCK, BLOCK), 0) >= lax.broadcasted_iota(
        jnp.int32, (BLOCK, BLOCK), 1
    )
    raw_scores = jnp.einsum(
        "bthd,bshd->bhts", q_blocks, k_blocks, preferred_element_type=jnp.float32
    )
    scores = jnp.where(causal_mask, raw_scores * score_scale, 0.0).astype(jnp.bfloat16)
    intra = jnp.einsum("bhts,bshe->bthe", scores, v_blocks, preferred_element_type=jnp.float32)
    carried = jnp.einsum(
        "bthd,bhde->bthe", q_blocks, prefix_state, preferred_element_type=jnp.float32
    )
    attn_out = (intra + score_scale * carried).astype(jnp.bfloat16).reshape(tok_rows, col_count)
    raw_grad = jnp.einsum("bthe,bshe->bhts", g_blocks, v_blocks, preferred_element_type=jnp.float32)
    grad_scores = jnp.where(causal_mask, raw_grad * score_scale, 0.0).astype(jnp.bfloat16)
    grad_q = jnp.einsum(
        "bhts,bshd->bthd", grad_scores, k_blocks, preferred_element_type=jnp.float32
    ) + score_scale * jnp.einsum(
        "bthe,bhde->bthd", g_blocks, prefix_state, preferred_element_type=jnp.float32
    )
    grad_k = jnp.einsum(
        "bhts,bthd->bshd", grad_scores, q_blocks, preferred_element_type=jnp.float32
    ) + score_scale * jnp.einsum(
        "bshe,bhde->bshd", v_blocks, suffix_state, preferred_element_type=jnp.float32
    )
    grad_v = jnp.einsum(
        "bhts,bthe->bshe", scores, g_blocks, preferred_element_type=jnp.float32
    ) + score_scale * jnp.einsum(
        "bshd,bhde->bshe", k_blocks, suffix_state, preferred_element_type=jnp.float32
    )
    grad_q = grad_q.astype(jnp.bfloat16).reshape(tok_rows, col_count)
    grad_k = grad_k.astype(jnp.bfloat16).reshape(tok_rows, col_count)
    grad_v = grad_v.astype(jnp.bfloat16).reshape(tok_rows, col_count)
    partial_input = jnp.einsum("tc,dc->td", grad_q, full_query, preferred_element_type=jnp.float32)
    partial_input = partial_input + jnp.einsum(
        "tc,dc->td", grad_k, full_key, preferred_element_type=jnp.float32
    )
    partial_input = partial_input + jnp.einsum(
        "tc,dc->td", grad_v, full_value, preferred_element_type=jnp.float32
    )
    grad_x = lax.psum_scatter(
        partial_input.astype(jnp.bfloat16), "head", scatter_dimension=1, tiled=True
    )
    term_query = jnp.einsum("td,tc->dc", tokens, grad_q, preferred_element_type=jnp.float32)
    term_key = jnp.einsum("td,tc->dc", tokens, grad_k, preferred_element_type=jnp.float32)
    term_value = jnp.einsum("td,tc->dc", tokens, grad_v, preferred_element_type=jnp.float32)
    sum_query, sum_key, sum_value = (
        lax.psum_scatter(
            term_query.astype(jnp.bfloat16), "seq", scatter_dimension=0, tiled=True
        ).astype(jnp.float32),
        lax.psum_scatter(
            term_key.astype(jnp.bfloat16), "seq", scatter_dimension=0, tiled=True
        ).astype(jnp.float32),
        lax.psum_scatter(
            term_value.astype(jnp.bfloat16), "seq", scatter_dimension=0, tiled=True
        ).astype(jnp.float32),
    )
    grad_wq = sum_query.astype(jnp.bfloat16)
    grad_wk = sum_key.astype(jnp.bfloat16)
    grad_wv = sum_value.astype(jnp.bfloat16)
    return (attn_out, grad_x, grad_wq, grad_wk, grad_wv)


def head_attention(queries, keys, values, grads, score_scale):
    head_count = queries.shape[1] // HD
    q_blocks = split_blocks(queries, head_count)
    k_blocks = split_blocks(keys, head_count)
    v_blocks = split_blocks(values, head_count)
    g_blocks = split_blocks(grads, head_count)
    f32 = jnp.float32
    kv_blocks = jnp.einsum("bthd,bthe->bhde", k_blocks, v_blocks, preferred_element_type=f32)
    qg_blocks = jnp.einsum("bthd,bthe->bhde", q_blocks, g_blocks, preferred_element_type=f32)
    zero_state = jnp.zeros_like(kv_blocks[0])
    prefix_state = before_blocks(kv_blocks, zero_state).astype(jnp.bfloat16)
    suffix_state = after_blocks(qg_blocks, zero_state).astype(jnp.bfloat16)
    causal_mask = lax.broadcasted_iota(jnp.int32, (BLOCK, BLOCK), 0) >= lax.broadcasted_iota(
        jnp.int32, (BLOCK, BLOCK), 1
    )
    raw_scores = jnp.einsum("bthd,bshd->bhts", q_blocks, k_blocks, preferred_element_type=f32)
    scores = jnp.where(causal_mask, raw_scores * score_scale, 0.0).astype(jnp.bfloat16)
    raw_grad = jnp.einsum("bthe,bshe->bhts", g_blocks, v_blocks, preferred_element_type=f32)
    grad_scores = jnp.where(causal_mask, raw_grad * score_scale, 0.0).astype(jnp.bfloat16)

    def close(within, across):
        return (within + score_scale * across).astype(jnp.bfloat16).reshape(queries.shape)

    attn_out = close(
        jnp.einsum("bhts,bshe->bthe", scores, v_blocks, preferred_element_type=f32),
        jnp.einsum("bthd,bhde->bthe", q_blocks, prefix_state, preferred_element_type=f32),
    )
    grad_q = close(
        jnp.einsum("bhts,bshd->bthd", grad_scores, k_blocks, preferred_element_type=f32),
        jnp.einsum("bthe,bhde->bthd", g_blocks, prefix_state, preferred_element_type=f32),
    )
    grad_k = close(
        jnp.einsum("bhts,bthd->bshd", grad_scores, q_blocks, preferred_element_type=f32),
        jnp.einsum("bshe,bhde->bshd", v_blocks, suffix_state, preferred_element_type=f32),
    )
    grad_v = close(
        jnp.einsum("bhts,bthe->bshe", scores, g_blocks, preferred_element_type=f32),
        jnp.einsum("bshd,bhde->bshe", k_blocks, suffix_state, preferred_element_type=f32),
    )
    return attn_out, grad_q, grad_k, grad_v


def columns_first(matrix, parts):
    return jnp.transpose(matrix.reshape(matrix.shape[0], parts, -1), (1, 0, 2))


def columns_last(pieces):
    return jnp.transpose(pieces, (1, 0, 2)).reshape(pieces.shape[1], -1)


BOTH = ("seq", "head")
Z1, Z0, X, Y, CORE = 16, 8, 4, 2, 1


def swap(value, bit):
    count = lax.axis_size("seq") * lax.axis_size("head")
    return lax.ppermute(value, BOTH, [(i, i ^ bit) for i in range(count)])


def gather_rows(piece, bits):
    for bit in bits[:-1]:
        piece = jnp.concatenate([piece, swap(piece, bit)], axis=0)
    return [piece, swap(piece, bits[-1])]


def block_places(me, bits):
    index = jnp.arange(1 << len(bits), dtype=jnp.int32)
    place = jnp.zeros_like(index)
    for k, bit in enumerate(bits):
        place = place + ((index >> k) & 1) * bit
    return place ^ me


def joined(mine, theirs):
    return (mine.astype(jnp.float32) + theirs.astype(jnp.float32)).astype(jnp.bfloat16)


def fold(value, bit):
    half = value.shape[0] // 2
    return joined(value[:half], swap(value[half:], bit))


def select_rows(source_row, wanted_row, matrix):
    chosen = (wanted_row[:, None] == source_row[None, :]).astype(jnp.bfloat16)
    return jnp.dot(chosen, matrix, preferred_element_type=jnp.float32).astype(jnp.bfloat16)


def per_head(tokens, w_query, w_key, w_value, grad_out):
    seq_count, head_axis = lax.axis_size("seq"), lax.axis_size("head")
    tok_rows, width = tokens.shape
    weight_rows, col_count = w_query.shape
    own = col_count // seq_count
    tok_count = tok_rows * seq_count
    score_scale = 1.0 / math.sqrt(HD * tok_count)
    share = tok_rows // head_axis
    seat = lax.axis_index("head")
    me = lax.axis_index("seq") * head_axis + seat
    mine = lax.dynamic_slice_in_dim(tokens, seat * share, share, 0)

    orders = ((Z1, Z0, X, Y, CORE), (Z1, Z0, Y, X, CORE))
    part = share // 2
    pieces, gathered_row = [], []
    for k, bits in enumerate(orders):
        pieces += gather_rows(mine[k * part : (k + 1) * part], bits)
        starts = block_places(me, bits) * share + k * part
        gathered_row.append((starts[:, None] + jnp.arange(part)[None, :]).reshape(-1))
    gathered_row = jnp.concatenate(gathered_row)

    weights = jnp.concatenate(
        [columns_first(w, seq_count) for w in (w_query, w_key, w_value)], axis=2
    )
    weights = lax.all_to_all(weights, "seq", 0, 0, tiled=True).reshape(width, 3 * own)
    grads = lax.all_to_all(columns_first(grad_out, seq_count), "seq", 0, 0, tiled=True)
    grads = grads.reshape(tok_count, own)
    projected = jnp.concatenate(
        [
            jnp.dot(p, weights, preferred_element_type=jnp.float32).astype(jnp.bfloat16)
            for p in pieces
        ],
        axis=0,
    )
    rows = jnp.arange(tok_count, dtype=jnp.int32)
    projected = select_rows(gathered_row, rows, projected)
    attn_out, grad_q, grad_k, grad_v = head_attention(
        projected[:, :own], projected[:, own : 2 * own], projected[:, 2 * own :], grads, score_scale
    )
    attn_out = columns_last(
        lax.all_to_all(attn_out.reshape(seq_count, tok_rows, own), "seq", 0, 0, tiled=True)
    )
    gradient = jnp.concatenate([grad_q, grad_k, grad_v], axis=1)

    half_rows = tok_rows // 2
    seq_starts = (block_places(me, (Z1, Z0, X)) // head_axis) * tok_rows
    half_starts = jnp.concatenate([seq_starts, seq_starts + half_rows])
    scattered_row = (half_starts[:, None] + jnp.arange(half_rows)[None, :]).reshape(-1)
    placed = select_rows(rows, scattered_row, gradient)

    def term(other):
        chosen = lax.dynamic_slice_in_dim(
            weights, (seat ^ other) * (width // head_axis), width // head_axis, 0
        )
        return jnp.einsum("tc,dc->td", placed, chosen, preferred_element_type=jnp.float32).astype(
            jnp.bfloat16
        )

    far = swap(term(Y | CORE), CORE)
    near = swap(term(CORE), CORE)
    far = joined(term(Y), far)
    near = joined(term(0), near)
    middle = tok_count // 2
    quarter = middle // 2
    first = joined(near[:middle], swap(far[:middle], Y))
    first = fold(first, X)
    second_far = joined(far[middle : middle + quarter], swap(far[middle + quarter :], X))
    second_near = joined(near[middle : middle + quarter], swap(near[middle + quarter :], X))
    second = joined(second_near, swap(second_far, Y))
    grad_x = jnp.concatenate([fold(fold(v, Z0), Z1) for v in (first, second)], axis=0)

    matching = select_rows(rows, gathered_row, gradient)
    grad_w, lower = 0.0, 0
    for p in pieces:
        grad_w = grad_w + jnp.einsum(
            "td,tc->dc", p, matching[lower : lower + p.shape[0]], preferred_element_type=jnp.float32
        )
        lower += p.shape[0]
    grad_w = lax.all_to_all(
        grad_w.astype(jnp.bfloat16).reshape(seq_count, weight_rows, 3 * own), "seq", 0, 0, tiled=True
    )
    grad_wq, grad_wk, grad_wv = (
        columns_last(grad_w[:, :, i * own : (i + 1) * own]) for i in range(3)
    )
    return (attn_out, grad_x, grad_wq, grad_wk, grad_wv)


def solution(mesh):
    in_specs = (
        P("seq", None),
        P("seq", "head"),
        P("seq", "head"),
        P("seq", "head"),
        P("seq", "head"),
    )
    out_specs = (
        P("seq", "head"),
        P("seq", "head"),
        P("seq", "head"),
        P("seq", "head"),
        P("seq", "head"),
    )

    def whole(tokens, w_query, w_key, w_value, grad_out):
        seq_count, head_axis = mesh.shape["seq"], mesh.shape["head"]
        heads = w_query.shape[1] // HD
        even = (seq_count, head_axis) == (8, 4) and heads % (seq_count * head_axis) == 0
        return mapped(per_head if even else per_device)(tokens, w_query, w_key, w_value, grad_out)

    def mapped(body):
        return jax.shard_map(
            body, mesh=mesh, in_specs=in_specs, out_specs=out_specs, check_vma=False
        )

    return whole
```
